32 devices in a mesh: grp: 4 (over y, x), seq: 8 (over z, core).
Axes of the slice: x: 2, y: 2, z: 4, core: 2. Of those that a mesh axis runs over, the one named last changes fastest.
Arguments:
- passage_q: bfloat16 [16384, 4096], P(('grp', 'seq')), may hold values from -8 to 8
- passage_k: bfloat16 [16384, 512], P(('grp', 'seq')), may hold values from -8 to 8
- passage_v: bfloat16 [16384, 512], P(('grp', 'seq')), may hold values from -6 to 6
- kept: int32 [32, 4], P(('grp', 'seq')), may hold values from 0 to 1, as said below
- context_map: int32 [4, 8], P('grp', 'seq'), may hold values from 0 to 31, as said below
- recompute_pos: int32 [4, 512], P('grp', 'seq'), may hold values from 0 to 4095, as said below
- recompute_q: bfloat16 [4, 512, 4096], P('grp', 'seq'), may hold values from -8 to 8
- recompute_k: bfloat16 [4, 512, 512], P('grp', 'seq'), may hold values from -8 to 8
- recompute_v: bfloat16 [4, 512, 512], P('grp', 'seq'), may hold values from -6 to 6
Outputs:
- passage_out: bfloat16 [16384, 4096], P(('grp', 'seq'))
- reader_out: bfloat16 [4, 512, 4096], P('grp', 'seq')
The draws below stay inside these ranges and needn't reach their ends.
Inputs may be any that keep to these rules, and one draw needn't show every extreme that they name: Block 0 of every passage is kept; a passage keeps at most 3 of its 4 blocks, and some passage keeps exactly 3. `context_map`: every passage appears exactly once. Entry [g, s] names a passage encoded on a device whose seq index is s. `recompute_pos`: entries [g, s * 64] to [g, (s + 1) * 64 - 1] are distinct ascending positions from s * 512 to (s + 1) * 512 - 1.
All inputs are finite; a program needn't handle non-finite values.
Results may differ from the reference program's by a relative error of at most 0.005.
Values may be sent and summed in bfloat16 or wider, within the bound.
A program may use at most 256 MiB of HBM per device.

```python
import jax
import jax.numpy as jnp
from jax import lax

HQ = 32
KVH = 4
HD = 128
PLEN = 512
BLK = 128
KEEP = 3
PASS_DEV = 1
NBLK = 4
NPASS = 32
CTX_LEN = 4096
R_DEV = 64
RECOMP = 512
N_GRP = 4
N_SEQ = 8


def query_draw(key, salt, shape):
    subkey = jax.random.fold_in(key, salt)
    values = jnp.clip(jax.random.normal(subkey, shape, jnp.float32), -6.0, 6.0)
    return values.astype(jnp.bfloat16)


def key_draw(key, salt, shape):
    subkey = jax.random.fold_in(key, salt)
    values = jnp.clip(2.5 * jax.random.normal(subkey, shape, jnp.float32), -7.5, 7.5)
    return values.astype(jnp.bfloat16)


def draw_passage_q(key, part):
    return query_draw(key, 11, (NPASS * PLEN, HQ * HD))


def draw_passage_k(key, part):
    return key_draw(key, 21, (NPASS * PLEN, KVH * HD))


def draw_recompute_q(key, part):
    return query_draw(key, 31, (N_GRP, RECOMP, HQ * HD))


def draw_recompute_k(key, part):
    return key_draw(key, 41, (N_GRP, RECOMP, KVH * HD))


def draw_kept(key, part):
    extra = jax.random.randint(jax.random.fold_in(key, 51), (NPASS,), 0, KEEP)
    extra = extra.at[0].set(KEEP - 1)
    subkeys = jax.random.split(jax.random.fold_in(key, 52), NPASS)
    ranking = jax.vmap(lambda subkey: jax.random.permutation(subkey, NBLK - 1))(subkeys)
    others = (ranking < extra[:, None]).astype(jnp.int32)
    return jnp.concatenate([jnp.ones((NPASS, 1), jnp.int32), others], axis=1)


def draw_context_map(key, part):
    column_size = N_GRP * PASS_DEV
    subkeys = jax.random.split(jax.random.fold_in(key, 61), N_SEQ)
    orders = jax.vmap(lambda subkey: jax.random.permutation(subkey, column_size))(subkeys)
    chosen = orders.reshape(N_SEQ, N_GRP, PASS_DEV).transpose(1, 0, 2)
    source_group = chosen // PASS_DEV
    source_slot = chosen % PASS_DEV
    column_index = jnp.arange(N_SEQ).reshape(1, N_SEQ, 1)
    passage_ids = (source_group * N_SEQ + column_index) * PASS_DEV + source_slot
    return passage_ids.reshape(N_GRP, N_SEQ * PASS_DEV).astype(jnp.int32)


def draw_recompute_pos(key, part):
    span_rows = PASS_DEV * PLEN
    subkeys = jax.random.split(jax.random.fold_in(key, 71), N_GRP * N_SEQ)
    picked = jax.vmap(lambda subkey: jnp.sort(jax.random.permutation(subkey, span_rows)[:R_DEV]))(subkeys)
    starts = jnp.arange(N_GRP * N_SEQ) % N_SEQ * span_rows
    return (picked + starts[:, None]).reshape(N_GRP, RECOMP).astype(jnp.int32)


def levels(own_key, extent, pieces, low, high):
    level = 1.0
    for dim, parts in pieces:
        steps = jax.random.uniform(jax.random.fold_in(jax.random.fold_in(own_key, 6), dim), (parts,), jnp.float32, low / len(pieces), high / len(pieces))
        level = level * jnp.repeat(jnp.exp(steps), extent[dim] // parts).reshape((-1,) + (1,) * (len(extent) - 1 - dim))
    return level


def bell_draw(own_key, dims, width, reach, cuts=(), held_as=jnp.bfloat16):
    factor_of = levels(own_key, dims, cuts, -0.22, 0.18) if cuts else 1.0
    result = jax.random.normal(own_key, dims, jnp.float32) * width * factor_of
    return jnp.minimum(jnp.maximum(result, -reach), reach).astype(held_as)


def setup_inputs(seed: int = 0) -> dict:
    streams_of = jax.random.split(jax.random.key(seed), 10)
    passage_q = draw_passage_q(jax.random.fold_in(streams_of[9], 71), 0)
    passage_k = draw_passage_k(jax.random.fold_in(streams_of[9], 71), 0)
    passage_v = bell_draw(streams_of[2], (NPASS * PLEN, KVH * HD), 1.0, 6.0, ((0, 32),))
    kept = draw_kept(jax.random.fold_in(streams_of[9], 71), 0)
    context_map = draw_context_map(jax.random.fold_in(streams_of[9], 71), 0)
    recompute_pos = draw_recompute_pos(jax.random.fold_in(streams_of[9], 71), 0)
    recompute_q = draw_recompute_q(jax.random.fold_in(streams_of[9], 71), 0)
    recompute_k = draw_recompute_k(jax.random.fold_in(streams_of[9], 71), 0)
    recompute_v = bell_draw(streams_of[8], (N_GRP, RECOMP, KVH * HD), 1.0, 6.0, ((0, 4), (1, 8)))
    return {"passage_q": passage_q, "passage_k": passage_k, "passage_v": passage_v, "kept": kept, "context_map": context_map, "recompute_pos": recompute_pos, "recompute_q": recompute_q, "recompute_k": recompute_k, "recompute_v": recompute_v}


def passage_attention(queries, key_rows, value_rows):
    length = queries.shape[0]
    query_heads = queries.astype(jnp.float32).reshape(length, KVH, HQ // KVH, HD)
    key_heads = key_rows.astype(jnp.float32).reshape(length, KVH, HD)
    value_heads = value_rows.astype(jnp.float32).reshape(length, KVH, HD)
    scores = jnp.einsum('ikgd,jkd->kgij', query_heads, key_heads) * (HD ** -0.5)
    causal = jnp.arange(length)[:, None] >= jnp.arange(length)[None, :]
    scores = jnp.where(causal, scores, -jnp.inf)
    maximum = jnp.max(scores, axis=-1, keepdims=True)
    weights = jnp.exp(scores - maximum).astype(jnp.bfloat16)
    totals = jnp.sum(weights.astype(jnp.float32), axis=-1)
    mixture = jnp.einsum('kgij,jkd->ikgd', weights.astype(jnp.float32), value_heads)
    mixture = mixture / jnp.moveaxis(totals, -1, 0)[..., None]
    return mixture.reshape(length, HQ * HD).astype(jnp.bfloat16)


def encode_items(items):
    return passage_attention(items[0], items[1], items[2])


def reader_group(passage_k, passage_v, kept, slot_map, positions, queries, own_keys, own_values):
    context_keys = passage_k.reshape(NPASS, PLEN, KVH * HD)[slot_map].reshape(CTX_LEN, KVH, HD).astype(jnp.float32)
    context_values = passage_v.reshape(NPASS, PLEN, KVH * HD)[slot_map].reshape(CTX_LEN, KVH, HD).astype(jnp.float32)
    kept_rows = jnp.repeat(kept[slot_map], BLK, axis=1).reshape(CTX_LEN)
    key_pos = jnp.arange(CTX_LEN).astype(jnp.int32)
    query_block = 64
    block_total = RECOMP // query_block

    def attend(items):
        block_q, block_k, block_v, block_pos = items
        query_heads = block_q.astype(jnp.float32).reshape(query_block, KVH, HQ // KVH, HD)
        own_k = block_k.astype(jnp.float32).reshape(query_block, KVH, HD)
        own_v = block_v.astype(jnp.float32).reshape(query_block, KVH, HD)
        scores = jnp.einsum('rkgd,nkd->rkgn', query_heads, context_keys) * (HD ** -0.5)
        visible = (kept_rows[None, :] > 0) & (key_pos[None, :] < block_pos[:, None])
        scores = jnp.where(visible[:, None, None, :], scores, -jnp.inf)
        own_score = jnp.einsum('rkgd,rkd->rkg', query_heads, own_k) * (HD ** -0.5)
        maximum = jnp.maximum(jnp.max(scores, axis=-1), own_score)
        weights = jnp.exp(scores - maximum[..., None]).astype(jnp.bfloat16)
        own_weight = jnp.exp(own_score - maximum).astype(jnp.bfloat16).astype(jnp.float32)
        totals = jnp.sum(weights.astype(jnp.float32), axis=-1) + own_weight
        mixture = jnp.einsum('rkgn,nkd->rkgd', weights.astype(jnp.float32), context_values)
        mixture = mixture + own_weight[..., None] * own_v[:, :, None, :]
        return (mixture / totals[..., None]).reshape(query_block, HQ * HD).astype(jnp.bfloat16)

    items = (queries.reshape(block_total, query_block, HQ * HD), own_keys.reshape(block_total, query_block, KVH * HD), own_values.reshape(block_total, query_block, KVH * HD), positions.reshape(block_total, query_block))
    return lax.map(attend, items).reshape(RECOMP, HQ * HD)


def reference(passage_q, passage_k, passage_v, kept, context_map, recompute_pos, recompute_q, recompute_k, recompute_v):
    items = (passage_q.reshape(NPASS, PLEN, HQ * HD), passage_k.reshape(NPASS, PLEN, KVH * HD), passage_v.reshape(NPASS, PLEN, KVH * HD))
    passage_out = lax.map(encode_items, items).reshape(NPASS * PLEN, HQ * HD)
    groups = []
    for group_index in range(N_GRP):
        groups.append(reader_group(passage_k, passage_v, kept, context_map[group_index], recompute_pos[group_index], recompute_q[group_index], recompute_k[group_index], recompute_v[group_index]))
    reader_out = jnp.stack(groups)
    return passage_out, reader_out
```

```python
import functools
import math

import jax
import jax.numpy as jnp
from jax import lax
from jax.experimental import pallas as pl
from jax.experimental.pallas import tpu as pltpu
from jax.sharding import PartitionSpec as P

HQ = 32
KVH = 4
HD = 128
PLEN = 512
BLK = 128
KEEP = 3
NBLK = PLEN // BLK
ROWS = KEEP * BLK
GQ = HQ // KVH
WKV = KVH * HD
QB = 256
SCALE2 = HD ** (-0.5) * math.log2(math.e)
NEG = -1e30


def dot_nt(a, b):
    return lax.dot_general(a, b, (((1,), (1,)), ((), ())), preferred_element_type=jnp.float32)


def with_ones(values):
    return jnp.concatenate([values, jnp.ones_like(values)], axis=1)


def passage_head(queries, keys, values_ones, first):
    number = first + QB
    scores = dot_nt(queries, keys[:number])
    row = lax.broadcasted_iota(jnp.int32, (QB, QB), 0)
    col = lax.broadcasted_iota(jnp.int32, (QB, QB), 1)
    diagonal = jnp.where(row >= col, scores[:, first:], NEG)
    scores = diagonal if first == 0 else jnp.concatenate([scores[:, :first], diagonal], axis=1)
    maximum = jnp.max(scores, axis=-1, keepdims=True)
    weights = jnp.exp2((scores - maximum) * SCALE2).astype(jnp.bfloat16)
    mixture = jnp.dot(weights, values_ones[:number], preferred_element_type=jnp.float32)
    return (mixture[:, :HD] / mixture[:, HD:]).astype(jnp.bfloat16)


def passage_kernel(q_ref, k_ref, v_ref, out_ref):
    keys = k_ref[...]
    values_ones = with_ones(v_ref[...])
    for head in range(GQ):
        cols = slice(head * HD, (head + 1) * HD)
        for first in range(0, PLEN, QB):
            rows = slice(first, first + QB)
            out_ref[rows, cols] = passage_head(q_ref[rows, cols], keys, values_ones, first)


def reader_kernel(q_ref, ok_ref, ov_ref, bias_ref, k_ref, v_ref, out_ref, m_ref, acc_ref):
    count = q_ref.shape[0]
    me = lax.axis_index("seq")
    own_k = ok_ref[...].astype(jnp.float32)
    own_v = ov_ref[...].astype(jnp.float32)
    queries = jnp.concatenate(
        [q_ref[:, h * HD : (h + 1) * HD] for h in range(GQ)], axis=0
    )
    own_tiled = jnp.concatenate([own_k] * GQ, axis=0)
    own_score = jnp.sum(queries.astype(jnp.float32) * own_tiled, axis=-1, keepdims=True)
    m_ref[...] = jnp.broadcast_to(own_score, m_ref.shape)
    acc_ref[:, :HD] = jnp.concatenate([own_v] * GQ, axis=0)
    acc_ref[:, HD:] = jnp.ones((GQ * count, HD), jnp.float32)

    def shard(index, carry):
        scores = dot_nt(queries, k_ref[index])
        bias = bias_ref[index]
        scores = scores + jnp.concatenate([bias] * GQ, axis=0)
        old = m_ref[...]
        new = jnp.maximum(old, jnp.max(scores, axis=-1, keepdims=True))
        factor = jnp.exp2((old - new) * SCALE2)
        weights = jnp.exp2(
            (scores - jnp.concatenate([new] * KEEP, axis=1)) * SCALE2
        ).astype(jnp.bfloat16)
        mixture = jnp.dot(weights, with_ones(v_ref[index]), preferred_element_type=jnp.float32)
        acc_ref[...] = acc_ref[...] * jnp.concatenate([factor, factor], axis=1) + mixture
        m_ref[...] = new
        return carry

    lax.fori_loop(0, me + 1, shard, 0)
    result = (acc_ref[:, :HD] / acc_ref[:, HD:]).astype(out_ref.dtype)
    for h in range(GQ):
        out_ref[:, h * HD : (h + 1) * HD] = result[h * count : (h + 1) * count]


def on_device(passage_q, passage_k, passage_v, kept, context_map, recompute_pos,
              recompute_q, recompute_k, recompute_v):
    groups = lax.axis_size("grp")
    seqs = lax.axis_size("seq")
    count = recompute_q.shape[1]
    group = lax.axis_index("grp")
    column = lax.axis_index("seq")

    info = jnp.concatenate([kept, context_map], axis=1)
    everyone = lax.all_gather(info, ("grp", "seq"), axis=0, tiled=True)
    all_kept = everyone[:, :NBLK]
    my_map = lax.dynamic_slice_in_dim(everyone[:, NBLK], group * seqs, seqs)

    def block_ids(flags):
        ranking = jnp.cumsum(flags, axis=-1) - 1
        slots = jnp.arange(KEEP)
        chosen = (flags[..., None, :] > 0) & (ranking[..., None, :] == slots[:, None])
        return jnp.sum(chosen * (jnp.arange(NBLK) + 1), axis=-1) - 1

    own_ids = jnp.maximum(block_ids(kept)[0], 0)
    both = jnp.concatenate([passage_k, passage_v], axis=1).reshape(NBLK, BLK, 2 * WKV)
    send = both[own_ids].reshape(ROWS, 2 * WKV)
    pieces = lax.all_gather(send, "grp", axis=0)
    local = lax.dynamic_index_in_dim(pieces, context_map[0, 0] // seqs, 0, keepdims=False)
    gathered = lax.all_gather(local, "seq", axis=0)

    ids = block_ids(all_kept[my_map])
    start = jnp.arange(seqs)[:, None] * PLEN + ids * BLK
    position = start[:, :, None] + jnp.arange(BLK)
    position = jnp.where(ids[:, :, None] >= 0, position, 2**30).reshape(seqs, 1, ROWS)
    visible = position < recompute_pos[0][None, :, None]
    bias = jnp.where(visible, 0.0, NEG).astype(jnp.float32)

    passage_out = pl.pallas_call(
        passage_kernel,
        grid=(KVH,),
        in_specs=[
            pl.BlockSpec((PLEN, GQ * HD), lambda j: (0, j)),
            pl.BlockSpec((PLEN, HD), lambda j: (0, j)),
            pl.BlockSpec((PLEN, HD), lambda j: (0, j)),
        ],
        out_specs=pl.BlockSpec((PLEN, GQ * HD), lambda j: (0, j)),
        out_shape=jax.ShapeDtypeStruct((PLEN, HQ * HD), jnp.bfloat16),
        compiler_params=pltpu.CompilerParams(vmem_limit_bytes=40 * 2**20),
        cost_estimate=pl.CostEstimate(
            flops=8 * 10**9, bytes_accessed=9 * 10**6, transcendentals=6 * 10**6
        ),
    )(passage_q, passage_k, passage_v)

    reader_out = pl.pallas_call(
        reader_kernel,
        grid=(KVH,),
        in_specs=[
            pl.BlockSpec((count, GQ * HD), lambda j: (0, j)),
            pl.BlockSpec((count, HD), lambda j: (0, j)),
            pl.BlockSpec((count, HD), lambda j: (0, j)),
            pl.BlockSpec((seqs, count, ROWS), lambda j: (0, 0, 0)),
            pl.BlockSpec((seqs, ROWS, HD), lambda j: (0, 0, j)),
            pl.BlockSpec((seqs, ROWS, HD), lambda j: (0, 0, KVH + j)),
        ],
        out_specs=pl.BlockSpec((count, GQ * HD), lambda j: (0, j)),
        out_shape=jax.ShapeDtypeStruct((count, HQ * HD), jnp.bfloat16),
        scratch_shapes=[
            pltpu.VMEM((GQ * count, HD), jnp.float32),
            pltpu.VMEM((GQ * count, 2 * HD), jnp.float32),
        ],
        compiler_params=pltpu.CompilerParams(vmem_limit_bytes=40 * 2**20),
    )(recompute_q[0], recompute_k[0], recompute_v[0], bias, gathered, gathered)
    return passage_out, reader_out[None]


def solution(mesh):
    both = P(("grp", "seq"), None)
    rows = P("grp", "seq", None)
    return jax.shard_map(
        on_device,
        mesh=mesh,
        in_specs=(both, both, both, both, P("grp", "seq"), P("grp", "seq"), rows, rows, rows),
        out_specs=(both, rows),
        check_vma=False,
    )
```

```python
import functools
import math

import jax
import jax.numpy as jnp
from jax import lax
from jax.experimental import pallas as pl
from jax.experimental.pallas import tpu as pltpu
from jax.sharding import PartitionSpec as P

HQ = 32
KVH = 4
HD = 128
PLEN = 512
BLK = 128
KEEP = 3
NBLK = PLEN // BLK
ROWS = KEEP * BLK
GQ = HQ // KVH
WKV = KVH * HD
CORES = 2
HKV = KVH // CORES
HALF = WKV // CORES
HALFQ = HQ * HD // CORES
QB = 256
SCALE2 = HD ** (-0.5) * math.log2(math.e)
NEG = -1e30
FAR = 2**30
MESH = pl.DeviceIdType.MESH


def dot_nt(a, b):
    return lax.dot_general(a, b, (((1,), (1,)), ((), ())), preferred_element_type=jnp.float32)


def with_ones(values):
    return jnp.concatenate([values, jnp.ones_like(values)], axis=1)


def passage_head(queries, keys, values_ones, first):
    number = first + QB
    scores = dot_nt(queries, keys[:number])
    row = lax.broadcasted_iota(jnp.int32, (QB, QB), 0)
    col = lax.broadcasted_iota(jnp.int32, (QB, QB), 1)
    diagonal = jnp.where(row >= col, scores[:, first:], NEG)
    scores = diagonal if first == 0 else jnp.concatenate([scores[:, :first], diagonal], axis=1)
    maximum = jnp.max(scores, axis=-1, keepdims=True)
    weights = jnp.exp2((scores - maximum) * SCALE2).astype(jnp.bfloat16)
    mixture = jnp.dot(weights, values_ones[:number], preferred_element_type=jnp.float32)
    return (mixture[:, :HD] / mixture[:, HD:]).astype(jnp.bfloat16)


def kept_slots(flags):
    one, two, three = (flags[i] > 0 for i in range(1, NBLK))
    first = jnp.where(one, 1, jnp.where(two, 2, jnp.where(three, 3, -1)))
    second = jnp.where(
        one, jnp.where(two, 2, jnp.where(three, 3, -1)), jnp.where(two & three, 3, -1)
    )
    return [0, first, second]


def kernel(groups, seqs, kept_s, map_s, pq, pk, pv, qpos, rq, rk, rv, pout, rout,
           send_k, send_v, pool_k, pool_v, st_k, st_v, rec_k, rec_v, kv, pos, info, info_s,
           qb, ob, okb, ovb, qpb, m_ref, acc_ref, pbuf,
           info_ss, info_rs, s1s, s1r, s2s, s2r, chs, chr_, qs, qr, qls, osem, outs, isem):
    chips = seqs // CORES
    g = lax.axis_index("grp")
    s = lax.axis_index("seq")
    z, c = s // CORES, lax.rem(s, CORES)
    other = 1 - c
    gx = g + 1 - 2 * lax.rem(g, 2)
    gy = lax.rem(g + groups // 2, groups)
    base = z * CORES
    count = rq.shape[0]

    def device(group, seq):
        return {"grp": group, "seq": seq}

    def peers():
        for step in range(1, 2 * groups):
            dg, dc = step // CORES, step % CORES
            yield step, lax.rem(g + dg, groups), base + lax.rem(c + dc, CORES)

    barrier = pltpu.get_barrier_semaphore()
    for step, pg, ps in peers():
        pl.semaphore_signal(barrier, inc=1, device_id=device(pg, ps), device_id_type=MESH)

    @pl.when(z > 0)
    def _():
        pl.semaphore_signal(barrier, inc=1, device_id=device(g, s - CORES), device_id_type=MESH)

    @pl.when(z < chips - 1)
    def _():
        pl.semaphore_signal(barrier, inc=1, device_id=device(g, s + CORES), device_id_type=MESH)

    own_slots = kept_slots([kept_s[0, i] for i in range(NBLK)])
    for slot in range(KEEP):
        index = jnp.maximum(own_slots[slot], 0)
        for source, target in ((pk, send_k), (pv, send_v)):
            block = source[index]
            for h in range(CORES):
                target[h, slot * BLK : (slot + 1) * BLK] = block[:, h * HALF : (h + 1) * HALF]
    tile_row = lax.broadcasted_iota(jnp.int32, (8, 128), 0)
    tile = jnp.full((8, 128), map_s[0, 0], jnp.int32)
    for i in range(NBLK):
        tile = jnp.where(tile_row == i, kept_s[0, i], tile)
    me8 = g * CORES + c
    info[me8] = tile
    pool_k[0, c] = send_k[c]
    pool_v[0, c] = send_v[c]

    along = jnp.minimum(z, 1) + jnp.minimum(chips - 1 - z, 1)
    pl.semaphore_wait(barrier, 2 * groups - 1 + along)

    def remote(src, dst, ssem, rsem, group, seq):
        return pltpu.make_async_remote_copy(
            src_ref=src, dst_ref=dst, send_sem=ssem, recv_sem=rsem,
            device_id=device(group, seq), device_id_type=MESH,
        )

    info_copies = []
    for step, pg, ps in peers():
        copy = remote(info.at[me8], info.at[me8], info_ss.at[step], info_rs.at[me8], pg, ps)
        copy.start()
        info_copies.append(copy)

    stage1 = []
    for index, (send, pool, first) in enumerate(((send_k, pool_k, gx), (send_v, pool_v, gy))):
        for number, (pg, pc, near) in enumerate(((first, c, 1), (first, other, 1), (g, other, 0))):
            copy = remote(send.at[pc], pool.at[near, c], s1s.at[index, number],
                          s1r.at[index, near, c], pg, base + pc)
            copy.start()
            stage1.append(copy)

    half_q = pl.ds(pl.multiple_of(c * HALFQ, HALFQ), HALFQ)
    away_q = pl.ds(pl.multiple_of(other * HALFQ, HALFQ), HALFQ)
    half_k = pl.ds(pl.multiple_of(c * HALF, HALF), HALF)
    away_k = pl.ds(pl.multiple_of(other * HALF, HALF), HALF)
    own_views = ((rq.at[:, half_q], qb), (rk.at[:, half_k], okb), (rv.at[:, half_k], ovb), (qpos, qpb))
    away_views = ((rq.at[:, away_q], qb), (rk.at[:, away_k], okb), (rv.at[:, away_k], ovb), (qpos, qpb))
    q_local, q_remote = [], []
    for index, (src, buf) in enumerate(own_views):
        copy = pltpu.make_async_copy(src, buf.at[c], qls.at[index])
        copy.start()
        q_local.append(copy)
    for index, (src, buf) in enumerate(away_views):
        copy = remote(src, buf.at[c], qs.at[index], qr.at[index], g, base + other)
        copy.start()
        q_remote.append(copy)

    out_copies = []

    def passage(j):
        keys = jnp.concatenate([pk[b, :, j * HD : (j + 1) * HD] for b in range(NBLK)], axis=0)
        values = with_ones(
            jnp.concatenate([pv[b, :, j * HD : (j + 1) * HD] for b in range(NBLK)], axis=0)
        )

        def heads(pair, carry):
            for k in range(2):
                head = j * GQ + pair * 2 + k
                cols = pl.ds(pl.multiple_of(head * HD, HD), HD)
                for first in range(0, PLEN, QB):
                    rows = slice(first, first + QB)
                    pbuf[rows, cols] = passage_head(pq[rows, cols], keys, values, first)
            return carry

        lax.fori_loop(0, GQ // 2, heads, 0)
        cols = slice(j * GQ * HD, (j + 1) * GQ * HD)
        copy = pltpu.make_async_copy(pbuf.at[:, cols], pout.at[:, cols], outs.at[j])
        copy.start()
        out_copies.append(copy)

    passage(0)
    passage(1)

    for step, pg, ps in peers():
        them = pg * CORES + lax.rem(c + step % CORES, CORES)
        remote(info.at[them], info.at[them], info_ss.at[step], info_rs.at[them], pg, ps).wait_recv()
    scalars = pltpu.make_async_copy(info, info_s, isem)
    scalars.start()
    scalars.wait()
    stage2 = []
    for index, (send, pool, st, rec, first, second) in enumerate(
        ((send_k, pool_k, st_k, rec_k, gx, gy), (send_v, pool_v, st_v, rec_v, gy, gx))
    ):
        for near, cc in ((0, other), (1, 0), (1, 1)):
            remote(send.at[0], pool.at[near, cc], s1s.at[index, 0], s1r.at[index, near, cc],
                   first, s).wait_recv()
        for cc in range(CORES):
            source = info_s[second * CORES + cc, NBLK, 0] // seqs
            st[cc] = pool[jnp.where(source == first, 1, 0), cc]
        copy = remote(st, rec, s2s.at[index], s2r.at[index], second, s)
        copy.start()
        stage2.append(copy)

    passage(2)

    for index, (pool, rec, copy, first) in enumerate(
        ((pool_k, rec_k, stage2[0], gx), (pool_v, rec_v, stage2[1], gy))
    ):
        copy.wait_recv()
        for cc in range(CORES):
            source = info_s[g * CORES + cc, NBLK, 0] // seqs
            near = pool[jnp.where(source == first, 1, 0), cc]
            here = (source == g) | (source == first)
            kv[z, index, cc * ROWS : (cc + 1) * ROWS] = jnp.where(here, near, rec[cc])
    offset = lax.broadcasted_iota(jnp.int32, (8, BLK), 1)
    for cc in range(CORES):
        wanted = info_s[g * CORES + cc, NBLK, 0] // seqs
        slots = kept_slots([info_s[wanted * CORES + cc, i, 0] for i in range(NBLK)])
        for slot in range(KEEP):
            begin = jnp.where(slots[slot] >= 0, (base + cc) * PLEN + slots[slot] * BLK, FAR)
            first_lane = cc * ROWS + slot * BLK
            pos[z, :, first_lane : first_lane + BLK] = offset + begin

    def chain(zz):
        return (
            remote(kv.at[zz], kv.at[zz], chs.at[zz, 0], chr_.at[zz, 0], g, lax.rem(s + CORES, seqs)),
            remote(pos.at[zz], pos.at[zz], chs.at[zz, 1], chr_.at[zz, 1], g, lax.rem(s + CORES, seqs)),
        )

    def forward(zz):
        @pl.when(z < chips - 1)
        def _():
            for copy in chain(zz):
                copy.start()

    forward(z)
    passage(3)

    for copy in q_local:
        copy.wait()
    for copy in q_remote:
        copy.wait()
    queries_total = CORES * count

    def head_cols(j, h):
        return slice((j * GQ + h) * HD, (j * GQ + h + 1) * HD)

    def pair_queries(j, h):
        parts = [qb[cc, :, head_cols(j, h + k)] for k in range(2) for cc in range(CORES)]
        return jnp.concatenate(parts, axis=0)

    width = 2 * queries_total
    for j in range(HKV):
        cols = slice(j * HD, (j + 1) * HD)
        own_k = jnp.concatenate([okb[0, :, cols], okb[1, :, cols]] * 2, axis=0).astype(jnp.float32)
        own_v = jnp.concatenate([ovb[0, :, cols], ovb[1, :, cols]] * 2, axis=0).astype(jnp.float32)
        for h in range(0, GQ, 2):
            rows = slice(h * queries_total, h * queries_total + width)
            product = pair_queries(j, h).astype(jnp.float32) * own_k
            score = jnp.sum(product, axis=-1, keepdims=True)
            m_ref[j, rows] = jnp.broadcast_to(score, (width, HD))
            acc_ref[j, rows, :HD] = own_v
            acc_ref[j, rows, HD:] = jnp.ones((width, HD), jnp.float32)

    def absorb(zz):
        keys_pos = pos[zz, 0:1, :]
        query_pos = jnp.concatenate([qpb[0, :, 0:1], qpb[1, :, 0:1]], axis=0)
        bias = jnp.where(keys_pos < query_pos, 0.0, NEG).astype(jnp.float32)
        bias = jnp.concatenate([bias, bias], axis=0)
        for j in range(HKV):
            cols = slice(j * HD, (j + 1) * HD)
            keys = kv[zz, 0, :, cols]
            values = with_ones(kv[zz, 1, :, cols])
            for h in range(0, GQ, 2):
                rows = slice(h * queries_total, h * queries_total + width)
                scores = dot_nt(pair_queries(j, h), keys) + bias
                old = m_ref[j, rows]
                new = jnp.maximum(old, jnp.max(scores, axis=-1, keepdims=True))
                factor = jnp.exp2((old - new) * SCALE2)
                tiled = jnp.concatenate([new] * (CORES * KEEP), axis=1)
                weights = jnp.exp2((scores - tiled) * SCALE2).astype(jnp.bfloat16)
                mixture = jnp.dot(weights, values, preferred_element_type=jnp.float32)
                acc_ref[j, rows] = acc_ref[j, rows] * jnp.concatenate([factor, factor], axis=1) + mixture
                m_ref[j, rows] = new

    def visit(k, carry):
        zz = z - k

        @pl.when(k > 0)
        def _():
            for copy in chain(zz):
                copy.wait_recv()
            forward(zz)

        absorb(zz)
        return carry

    lax.fori_loop(0, z + 1, visit, 0)

    for j in range(HKV):
        for h in range(0, GQ, 2):
            rows = slice(h * queries_total, h * queries_total + width)
            result = (acc_ref[j, rows, :HD] / acc_ref[j, rows, HD:]).astype(jnp.bfloat16)
            for k in range(2):
                for cc in range(CORES):
                    first = k * queries_total + cc * count
                    ob[cc, :, head_cols(j, h + k)] = result[first : first + count]
    swap = remote(ob.at[other], ob.at[2], osem.at[0], osem.at[1], g, base + other)
    swap.start()
    mine = pltpu.make_async_copy(ob.at[c], rout.at[:, half_q], osem.at[2])
    mine.start()
    swap.wait_recv()
    theirs = pltpu.make_async_copy(ob.at[2], rout.at[:, away_q], osem.at[3])
    theirs.start()
    mine.wait()
    theirs.wait()
    swap.wait_send()

    for copy in out_copies:
        copy.wait()
    for copy in info_copies + stage1 + stage2:
        copy.wait_send()

    @pl.when(z < chips - 1)
    def _():
        def drain(zz, carry):
            for copy in chain(zz):
                copy.wait_send()
            return carry

        lax.fori_loop(0, z + 1, drain, 0)


def on_device(groups, seqs, passage_q, passage_k, passage_v, kept, context_map, recompute_pos,
              recompute_q, recompute_k, recompute_v):
    count = recompute_q.shape[1]
    chips = seqs // CORES
    bf, f32, i32 = jnp.bfloat16, jnp.float32, jnp.int32
    dma = pltpu.SemaphoreType.DMA
    query_pos = jnp.broadcast_to(recompute_pos[0][:, None], (count, HD))
    smem = pl.BlockSpec(memory_space=pltpu.SMEM)
    vmem = pl.BlockSpec(memory_space=pltpu.VMEM)
    hbm = pl.BlockSpec(memory_space=pl.ANY)
    half = (CORES, ROWS, HALF)
    heads_rows = GQ * CORES * count
    passage_out, reader_out = pl.pallas_call(
        functools.partial(kernel, groups, seqs),
        out_shape=(
            jax.ShapeDtypeStruct((PLEN, HQ * HD), bf),
            jax.ShapeDtypeStruct((count, HQ * HD), bf),
        ),
        in_specs=[smem, smem, vmem, vmem, vmem, vmem, hbm, hbm, hbm],
        out_specs=(hbm, hbm),
        scratch_shapes=[
            pltpu.VMEM(half, bf), pltpu.VMEM(half, bf),
            pltpu.VMEM((2,) + half, bf), pltpu.VMEM((2,) + half, bf),
            pltpu.VMEM(half, bf), pltpu.VMEM(half, bf),
            pltpu.VMEM(half, bf), pltpu.VMEM(half, bf),
            pltpu.VMEM((chips, 2, CORES * ROWS, HALF), bf),
            pltpu.VMEM((chips, 8, CORES * ROWS), i32),
            pltpu.VMEM((groups * CORES, 8, 128), i32),
            pltpu.SMEM((groups * CORES, 8, 128), i32),
            pltpu.VMEM((CORES, count, HALFQ), bf),
            pltpu.VMEM((CORES + 1, count, HALFQ), bf),
            pltpu.VMEM((CORES, count, HALF), bf),
            pltpu.VMEM((CORES, count, HALF), bf),
            pltpu.VMEM((CORES, count, HD), i32),
            pltpu.VMEM((HKV, heads_rows, HD), f32),
            pltpu.VMEM((HKV, heads_rows, 2 * HD), f32),
            pltpu.VMEM((PLEN, HQ * HD), bf),
            dma((2 * groups,)), dma((2 * groups,)),
            dma((2, 3)), dma((2, 2, CORES)),
            dma((2,)), dma((2,)),
            dma((chips, 2)), dma((chips, 2)),
            dma((4,)), dma((4,)), dma((4,)), dma((4,)), dma((KVH,)), dma,
        ],
        compiler_params=pltpu.CompilerParams(
            collective_id=0, has_side_effects=True, vmem_limit_bytes=56 * 2**20
        ),
        cost_estimate=pl.CostEstimate(
            flops=16 * 10**9, bytes_accessed=12 * 10**6, transcendentals=12 * 10**6
        ),
    )(
        kept, context_map, passage_q,
        passage_k.reshape(NBLK, BLK, WKV), passage_v.reshape(NBLK, BLK, WKV),
        query_pos, recompute_q[0], recompute_k[0], recompute_v[0],
    )
    return passage_out, reader_out[None]


def solution(mesh):
    both = P(("grp", "seq"), None)
    rows = P("grp", "seq", None)
    return jax.shard_map(
        functools.partial(on_device, mesh.shape["grp"], mesh.shape["seq"]),
        mesh=mesh,
        in_specs=(both, both, both, both, P("grp", "seq"), P("grp", "seq"), rows, rows, rows),
        out_specs=(both, rows),
        check_vma=False,
    )
```

```python
import functools
import math

import jax
import jax.numpy as jnp
from jax import lax
from jax.experimental import pallas as pl
from jax.experimental.pallas import tpu as pltpu
from jax.sharding import PartitionSpec as P

HQ = 32
KVH = 4
HD = 128
PLEN = 512
BLK = 128
KEEP = 3
NBLK = PLEN // BLK
ROWS = KEEP * BLK
GQ = HQ // KVH
WKV = KVH * HD
CORES = 2
HKV = KVH // CORES
HALF = WKV // CORES
HALFQ = HQ * HD // CORES
QB = 256
SCALE2 = HD ** (-0.5) * math.log2(math.e)
NEG = -1e30
FAR = 2**30
MESH = pl.DeviceIdType.MESH


def dot_nt(a, b):
    return lax.dot_general(a, b, (((1,), (1,)), ((), ())), preferred_element_type=jnp.float32)


def with_ones(values):
    return jnp.concatenate([values, jnp.ones_like(values)], axis=1)


def passage_head(queries, keys, values_ones, first):
    number = first + QB
    scores = dot_nt(queries, keys[:number])
    row = lax.broadcasted_iota(jnp.int32, (QB, QB), 0)
    col = lax.broadcasted_iota(jnp.int32, (QB, QB), 1)
    diagonal = jnp.where(row >= col, scores[:, first:], NEG)
    scores = diagonal if first == 0 else jnp.concatenate([scores[:, :first], diagonal], axis=1)
    maximum = jnp.max(scores, axis=-1, keepdims=True)
    weights = jnp.exp2((scores - maximum) * SCALE2).astype(jnp.bfloat16)
    mixture = jnp.dot(weights, values_ones[:number], preferred_element_type=jnp.float32)
    return (mixture[:, :HD] / mixture[:, HD:]).astype(jnp.bfloat16)


def kept_slots(flags):
    one, two, three = (flags[i] > 0 for i in range(1, NBLK))
    first = jnp.where(one, 1, jnp.where(two, 2, jnp.where(three, 3, -1)))
    second = jnp.where(
        one, jnp.where(two, 2, jnp.where(three, 3, -1)), jnp.where(two & three, 3, -1)
    )
    return [0, first, second]


def kernel(groups, seqs, kept_s, map_s, qpos_s, pq, pk, pv, rq, rk, rv, pout, rout,
           kv, pos, info, info_s,
           qb, ob, okb, ovb, qpb, m_ref, acc_ref, pbuf,
           info_ss, info_rs, s1s, s1r, s2s, s2r, chs, chr_, qs, qr, qls, osem, outs, isem, *stages):
    chips = seqs // CORES
    g = lax.axis_index("grp")
    s = lax.axis_index("seq")
    z, c = s // CORES, lax.rem(s, CORES)
    other = 1 - c
    gx = g + 1 - 2 * lax.rem(g, 2)
    gy = lax.rem(g + groups // 2, groups)
    base = z * CORES
    count = rq.shape[0]
    send, pool, staged, got = (
        [[stages[kind * 2 * HKV + index * HKV + j] for j in range(HKV)] for index in range(2)]
        for kind in range(4)
    )
    axes = ((gx, gy), (gy, gx))

    def device(group, seq):
        return {"grp": group, "seq": seq}

    def peers():
        for step in range(1, 2 * groups):
            dg, dc = step // CORES, step % CORES
            yield step, lax.rem(g + dg, groups), base + lax.rem(c + dc, CORES)

    barrier = pltpu.get_barrier_semaphore()
    for step, pg, ps in peers():
        pl.semaphore_signal(barrier, inc=1, device_id=device(pg, ps), device_id_type=MESH)

    @pl.when(z > 0)
    def _():
        pl.semaphore_signal(barrier, inc=1, device_id=device(g, s - CORES), device_id_type=MESH)

    @pl.when(z < chips - 1)
    def _():
        pl.semaphore_signal(barrier, inc=1, device_id=device(g, s + CORES), device_id_type=MESH)

    own_slots = kept_slots([kept_s[0, i] for i in range(NBLK)])
    for slot in range(KEEP):
        index = jnp.maximum(own_slots[slot], 0)
        for source, target in ((pk, send[0]), (pv, send[1])):
            block = source[index]
            for h in range(CORES):
                for j in range(HKV):
                    first = h * HALF + j * HD
                    target[j][h, slot * BLK : (slot + 1) * BLK] = block[:, first : first + HD]
    tile_row = lax.broadcasted_iota(jnp.int32, (8, 128), 0)
    tile = jnp.full((8, 128), map_s[0, 0], jnp.int32)
    for i in range(NBLK):
        tile = jnp.where(tile_row == i, kept_s[0, i], tile)
    me8 = g * CORES + c
    info[me8] = tile
    for index in range(2):
        for j in range(HKV):
            pool[index][j][0, c] = send[index][j][c]
    for i in range(count):
        qpb[c, i : i + 1, :] = jnp.full((1, HD), qpos_s[0, i], jnp.int32)

    along = jnp.minimum(z, 1) + jnp.minimum(chips - 1 - z, 1)
    pl.semaphore_wait(barrier, 2 * groups - 1 + along)

    def remote(src, dst, ssem, rsem, group, seq):
        return pltpu.make_async_remote_copy(
            src_ref=src, dst_ref=dst, send_sem=ssem, recv_sem=rsem,
            device_id=device(group, seq), device_id_type=MESH,
        )

    info_copies = []
    for step, pg, ps in peers():
        copy = remote(info.at[me8], info.at[me8], info_ss.at[step], info_rs.at[me8], pg, ps)
        copy.start()
        info_copies.append(copy)

    stage1, stage2 = [], []

    def start_first(j):
        for index in range(2):
            first = axes[index][0]
            for number, (pg, pc, near) in enumerate(((first, c, 1), (first, other, 1), (g, other, 0))):
                copy = remote(send[index][j].at[pc], pool[index][j].at[near, c],
                              s1s.at[j, index, number], s1r.at[j, index, near, c], pg, base + pc)
                copy.start()
                stage1.append(copy)

    def start_second(j):
        for index in range(2):
            first, second = axes[index]
            for near, cc in ((0, other), (1, 0), (1, 1)):
                remote(send[index][j].at[0], pool[index][j].at[near, cc], s1s.at[j, index, 0],
                       s1r.at[j, index, near, cc], first, s).wait_recv()
            for cc in range(CORES):
                source = info_s[second * CORES + cc, NBLK, 0] // seqs
                staged[index][j][cc] = pool[index][j][jnp.where(source == first, 1, 0), cc]
            copy = remote(staged[index][j], got[index][j], s2s.at[j, index], s2r.at[j, index], second, s)
            copy.start()
            stage2.append(copy)

    start_first(0)

    half_q = pl.ds(pl.multiple_of(c * HALFQ, HALFQ), HALFQ)
    away_q = pl.ds(pl.multiple_of(other * HALFQ, HALFQ), HALFQ)
    half_k = pl.ds(pl.multiple_of(c * HALF, HALF), HALF)
    away_k = pl.ds(pl.multiple_of(other * HALF, HALF), HALF)
    own_views = ((rq.at[:, half_q], qb), (rk.at[:, half_k], okb), (rv.at[:, half_k], ovb))
    away_views = ((rq.at[:, away_q], qb), (rk.at[:, away_k], okb), (rv.at[:, away_k], ovb), (qpb.at[c], qpb))
    q_local, q_remote = [], []
    for index, (src, buf) in enumerate(own_views):
        copy = pltpu.make_async_copy(src, buf.at[c], qls.at[index])
        copy.start()
        q_local.append(copy)
    for index, (src, buf) in enumerate(away_views):
        copy = remote(src, buf.at[c], qs.at[index], qr.at[index], g, base + other)
        copy.start()
        q_remote.append(copy)

    out_copies = []

    def passage(j):
        keys = jnp.concatenate([pk[b, :, j * HD : (j + 1) * HD] for b in range(NBLK)], axis=0)
        values = with_ones(
            jnp.concatenate([pv[b, :, j * HD : (j + 1) * HD] for b in range(NBLK)], axis=0)
        )

        def heads(pair, carry):
            for k in range(2):
                head = j * GQ + pair * 2 + k
                cols = pl.ds(pl.multiple_of(head * HD, HD), HD)
                for first in range(0, PLEN, QB):
                    rows = slice(first, first + QB)
                    pbuf[rows, cols] = passage_head(pq[rows, cols], keys, values, first)
            return carry

        lax.fori_loop(0, GQ // 2, heads, 0)
        cols = slice(j * GQ * HD, (j + 1) * GQ * HD)
        copy = pltpu.make_async_copy(pbuf.at[:, cols], pout.at[:, cols], outs.at[j])
        copy.start()
        out_copies.append(copy)

    passage(0)

    for step, pg, ps in peers():
        them = pg * CORES + lax.rem(c + step % CORES, CORES)
        remote(info.at[them], info.at[them], info_ss.at[step], info_rs.at[them], pg, ps).wait_recv()
    scalars = pltpu.make_async_copy(info, info_s, isem)
    scalars.start()
    scalars.wait()
    start_second(0)
    start_first(1)
    offset = lax.broadcasted_iota(jnp.int32, (8, BLK), 1)
    for cc in range(CORES):
        wanted = info_s[g * CORES + cc, NBLK, 0] // seqs
        slots = kept_slots([info_s[wanted * CORES + cc, i, 0] for i in range(NBLK)])
        for slot in range(KEEP):
            begin = jnp.where(slots[slot] >= 0, (base + cc) * PLEN + slots[slot] * BLK, FAR)
            first_lane = cc * ROWS + slot * BLK
            pos[z, :, first_lane : first_lane + BLK] = offset + begin

    def chain(zz, j):
        up = lax.rem(s + CORES, seqs)
        copies = [remote(kv.at[zz, j], kv.at[zz, j], chs.at[zz, j], chr_.at[zz, j], g, up)]
        if j == 0:
            copies.append(remote(pos.at[zz], pos.at[zz], chs.at[zz, HKV], chr_.at[zz, HKV], g, up))
        return copies

    def forward(zz, j):
        @pl.when(z < chips - 1)
        def _():
            for copy in chain(zz, j):
                copy.start()

    def finish_stage(j):
        for index in range(2):
            first = axes[index][0]
            stage2[2 * j + index].wait_recv()
            for cc in range(CORES):
                source = info_s[g * CORES + cc, NBLK, 0] // seqs
                near = pool[index][j][jnp.where(source == first, 1, 0), cc]
                here = (source == g) | (source == first)
                kv[z, j, index, cc * ROWS : (cc + 1) * ROWS] = jnp.where(here, near, got[index][j][cc])
        forward(z, j)

    passage(1)
    finish_stage(0)
    start_second(1)
    passage(2)
    finish_stage(1)
    passage(3)

    for copy in q_local:
        copy.wait()
    for copy in q_remote:
        copy.wait()
    queries_total = CORES * count

    def head_cols(j, h):
        return slice((j * GQ + h) * HD, (j * GQ + h + 1) * HD)

    def pair_queries(j, h):
        parts = [qb[cc, :, head_cols(j, h + k)] for k in range(2) for cc in range(CORES)]
        return jnp.concatenate(parts, axis=0)

    width = 2 * queries_total
    for j in range(HKV):
        cols = slice(j * HD, (j + 1) * HD)
        own_k = jnp.concatenate([okb[0, :, cols], okb[1, :, cols]] * 2, axis=0).astype(jnp.float32)
        own_v = jnp.concatenate([ovb[0, :, cols], ovb[1, :, cols]] * 2, axis=0).astype(jnp.float32)
        for h in range(0, GQ, 2):
            rows = slice(h * queries_total, h * queries_total + width)
            product = pair_queries(j, h).astype(jnp.float32) * own_k
            score = jnp.sum(product, axis=-1, keepdims=True)
            m_ref[j, rows] = jnp.broadcast_to(score, (width, HD))
            acc_ref[j, rows, :HD] = own_v
            acc_ref[j, rows, HD:] = jnp.ones((width, HD), jnp.float32)

    def absorb(zz, j):
        keys_pos = pos[zz, 0:1, :]
        query_pos = jnp.concatenate([qpb[0, :, 0:1], qpb[1, :, 0:1]], axis=0)
        bias = jnp.where(keys_pos < query_pos, 0.0, NEG).astype(jnp.float32)
        bias = jnp.concatenate([bias, bias], axis=0)
        keys = kv[zz, j, 0]
        values = with_ones(kv[zz, j, 1])
        for h in range(0, GQ, 2):
            rows = slice(h * queries_total, h * queries_total + width)
            scores = dot_nt(pair_queries(j, h), keys) + bias
            old = m_ref[j, rows]
            new = jnp.maximum(old, jnp.max(scores, axis=-1, keepdims=True))
            factor = jnp.exp2((old - new) * SCALE2)
            tiled = jnp.concatenate([new] * (CORES * KEEP), axis=1)
            weights = jnp.exp2((scores - tiled) * SCALE2).astype(jnp.bfloat16)
            mixture = jnp.dot(weights, values, preferred_element_type=jnp.float32)
            acc_ref[j, rows] = acc_ref[j, rows] * jnp.concatenate([factor, factor], axis=1) + mixture
            m_ref[j, rows] = new

    def visit(k, carry):
        zz = z - k

        for j in range(HKV):

            @pl.when(k > 0)
            def _():
                for copy in chain(zz, j):
                    copy.wait_recv()
                forward(zz, j)

            absorb(zz, j)
        return carry

    lax.fori_loop(0, z + 1, visit, 0)

    for j in range(HKV):
        for h in range(0, GQ, 2):
            rows = slice(h * queries_total, h * queries_total + width)
            result = (acc_ref[j, rows, :HD] / acc_ref[j, rows, HD:]).astype(jnp.bfloat16)
            for k in range(2):
                for cc in range(CORES):
                    first = k * queries_total + cc * count
                    ob[cc, :, head_cols(j, h + k)] = result[first : first + count]
    swap = remote(ob.at[other], ob.at[2], osem.at[0], osem.at[1], g, base + other)
    swap.start()
    mine = pltpu.make_async_copy(ob.at[c], rout.at[:, half_q], osem.at[2])
    mine.start()
    swap.wait_recv()
    theirs = pltpu.make_async_copy(ob.at[2], rout.at[:, away_q], osem.at[3])
    theirs.start()
    mine.wait()
    theirs.wait()
    swap.wait_send()

    for copy in out_copies:
        copy.wait()
    for copy in info_copies + stage1 + stage2:
        copy.wait_send()

    @pl.when(z < chips - 1)
    def _():
        def drain(zz, carry):
            for j in range(HKV):
                for copy in chain(zz, j):
                    copy.wait_send()
            return carry

        lax.fori_loop(0, z + 1, drain, 0)


def on_device(groups, seqs, passage_q, passage_k, passage_v, kept, context_map, recompute_pos,
              recompute_q, recompute_k, recompute_v):
    count = recompute_q.shape[1]
    chips = seqs // CORES
    bf, f32, i32 = jnp.bfloat16, jnp.float32, jnp.int32
    dma = pltpu.SemaphoreType.DMA
    smem = pl.BlockSpec(memory_space=pltpu.SMEM)
    vmem = pl.BlockSpec(memory_space=pltpu.VMEM)
    hbm = pl.BlockSpec(memory_space=pl.ANY)
    half = (CORES, ROWS, HD)
    heads_rows = GQ * CORES * count
    passage_out, reader_out = pl.pallas_call(
        functools.partial(kernel, groups, seqs),
        out_shape=(
            jax.ShapeDtypeStruct((PLEN, HQ * HD), bf),
            jax.ShapeDtypeStruct((count, HQ * HD), bf),
        ),
        in_specs=[smem, smem, smem, vmem, vmem, vmem, hbm, hbm, hbm],
        out_specs=(hbm, hbm),
        scratch_shapes=[
            pltpu.VMEM((chips, HKV, 2, CORES * ROWS, HD), bf),
            pltpu.VMEM((chips, 8, CORES * ROWS), i32),
            pltpu.VMEM((groups * CORES, 8, 128), i32),
            pltpu.SMEM((groups * CORES, 8, 128), i32),
            pltpu.VMEM((CORES, count, HALFQ), bf),
            pltpu.VMEM((CORES + 1, count, HALFQ), bf),
            pltpu.VMEM((CORES, count, HALF), bf),
            pltpu.VMEM((CORES, count, HALF), bf),
            pltpu.VMEM((CORES, count, HD), i32),
            pltpu.VMEM((HKV, heads_rows, HD), f32),
            pltpu.VMEM((HKV, heads_rows, 2 * HD), f32),
            pltpu.VMEM((PLEN, HQ * HD), bf),
            dma((2 * groups,)), dma((2 * groups,)),
            dma((HKV, 2, 3)), dma((HKV, 2, 2, CORES)),
            dma((HKV, 2)), dma((HKV, 2)),
            dma((chips, HKV + 1)), dma((chips, HKV + 1)),
            dma((4,)), dma((4,)), dma((4,)), dma((4,)), dma((KVH,)), dma,
        ]
        + [pltpu.VMEM(shape, bf) for shape in (half, (2,) + half, half, half) for _ in range(2 * HKV)],
        compiler_params=pltpu.CompilerParams(
            collective_id=0, has_side_effects=True, vmem_limit_bytes=56 * 2**20
        ),
        cost_estimate=pl.CostEstimate(
            flops=16 * 10**9, bytes_accessed=12 * 10**6, transcendentals=12 * 10**6
        ),
    )(
        kept, context_map, recompute_pos, passage_q,
        passage_k.reshape(NBLK, BLK, WKV), passage_v.reshape(NBLK, BLK, WKV),
        recompute_q[0], recompute_k[0], recompute_v[0],
    )
    return passage_out, reader_out[None]


def solution(mesh):
    both = P(("grp", "seq"), None)
    rows = P("grp", "seq", None)
    return jax.shard_map(
        functools.partial(on_device, mesh.shape["grp"], mesh.shape["seq"]),
        mesh=mesh,
        in_specs=(both, both, both, both, P("grp", "seq"), P("grp", "seq"), rows, rows, rows),
        out_specs=(both, rows),
        check_vma=False,
    )
```

```python
import functools
import math

import jax
import jax.numpy as jnp
from jax import lax
from jax.experimental import pallas as pl
from jax.experimental.pallas import tpu as pltpu
from jax.sharding import PartitionSpec as P

HQ = 32
KVH = 4
HD = 128
PLEN = 512
BLK = 128
KEEP = 3
NBLK = PLEN // BLK
ROWS = KEEP * BLK
GQ = HQ // KVH
WKV = KVH * HD
CORES = 2
HKV = KVH // CORES
HALF = WKV // CORES
HALFQ = HQ * HD // CORES
QB = 256
SCALE2 = HD ** (-0.5) * math.log2(math.e)
NEG = -1e30
FAR = 2**30
MESH = pl.DeviceIdType.MESH


def dot_nt(a, b):
    return lax.dot_general(a, b, (((1,), (1,)), ((), ())), preferred_element_type=jnp.float32)


def with_ones(values):
    return jnp.concatenate([values, jnp.ones_like(values)], axis=1)


def passage_head(queries, keys, values_ones, first):
    number = first + QB
    scores = dot_nt(queries, keys[:number])
    row = lax.broadcasted_iota(jnp.int32, (QB, QB), 0)
    col = lax.broadcasted_iota(jnp.int32, (QB, QB), 1)
    diagonal = jnp.where(row >= col, scores[:, first:], NEG)
    scores = diagonal if first == 0 else jnp.concatenate([scores[:, :first], diagonal], axis=1)
    maximum = jnp.max(scores, axis=-1, keepdims=True)
    weights = jnp.exp2((scores - maximum) * SCALE2).astype(jnp.bfloat16)
    mixture = jnp.dot(weights, values_ones[:number], preferred_element_type=jnp.float32)
    return (mixture[:, :HD] / mixture[:, HD:]).astype(jnp.bfloat16)


def kept_slots(flags):
    one, two, three = (flags[i] > 0 for i in range(1, NBLK))
    first = jnp.where(one, 1, jnp.where(two, 2, jnp.where(three, 3, -1)))
    second = jnp.where(
        one, jnp.where(two, 2, jnp.where(three, 3, -1)), jnp.where(two & three, 3, -1)
    )
    return [0, first, second]


def kernel(groups, seqs, kept_s, map_s, qpos_s, pq, pk, pv, rq, rk, rv, pout, rout,
           kv, pos, info, info_s,
           qb, ob, okb, ovb, qpb, m_ref, acc_ref, pbuf,
           info_ss, info_rs, s1s, s1r, s2s, s2r, chs, chr_, qs, qr, qls, osem, outs, isem, *stages):
    chips = seqs // CORES
    g = lax.axis_index("grp")
    s = lax.axis_index("seq")
    z, c = s // CORES, lax.rem(s, CORES)
    other = 1 - c
    gx = g + 1 - 2 * lax.rem(g, 2)
    gy = lax.rem(g + groups // 2, groups)
    base = z * CORES
    count = rq.shape[0]
    send, pool, staged, got = (
        [[stages[kind * 2 * HKV + index * HKV + j] for j in range(HKV)] for index in range(2)]
        for kind in range(4)
    )
    axes = ((gx, gy), (gy, gx))

    def device(group, seq):
        return {"grp": group, "seq": seq}

    def peers():
        for step in range(1, 2 * groups):
            dg, dc = step // CORES, step % CORES
            yield step, lax.rem(g + dg, groups), base + lax.rem(c + dc, CORES)

    barrier = pltpu.get_barrier_semaphore()
    for step, pg, ps in peers():
        pl.semaphore_signal(barrier, inc=1, device_id=device(pg, ps), device_id_type=MESH)

    @pl.when(z > 0)
    def _():
        pl.semaphore_signal(barrier, inc=1, device_id=device(g, s - CORES), device_id_type=MESH)

    @pl.when(z < chips - 1)
    def _():
        pl.semaphore_signal(barrier, inc=1, device_id=device(g, s + CORES), device_id_type=MESH)

    own_slots = kept_slots([kept_s[0, i] for i in range(NBLK)])
    for slot in range(KEEP):
        index = jnp.maximum(own_slots[slot], 0)
        for source, target in ((pk, send[0]), (pv, send[1])):
            block = source[index]
            for h in range(CORES):
                for j in range(HKV):
                    first = h * HALF + j * HD
                    target[j][h, slot * BLK : (slot + 1) * BLK] = block[:, first : first + HD]
    tile_row = lax.broadcasted_iota(jnp.int32, (8, 128), 0)
    tile = jnp.full((8, 128), map_s[0, 0], jnp.int32)
    for i in range(NBLK):
        tile = jnp.where(tile_row == i, kept_s[0, i], tile)
    me8 = g * CORES + c
    info[me8] = tile
    for index in range(2):
        for j in range(HKV):
            pool[index][j][0, c] = send[index][j][c]
    for i in range(count):
        qpb[c, i : i + 1, :] = jnp.full((1, HD), qpos_s[0, i], jnp.int32)

    along = jnp.minimum(z, 1) + jnp.minimum(chips - 1 - z, 1)
    pl.semaphore_wait(barrier, 2 * groups - 1 + along)

    def remote(src, dst, ssem, rsem, group, seq):
        return pltpu.make_async_remote_copy(
            src_ref=src, dst_ref=dst, send_sem=ssem, recv_sem=rsem,
            device_id=device(group, seq), device_id_type=MESH,
        )

    info_copies = []
    for step, pg, ps in peers():
        copy = remote(info.at[me8], info.at[me8], info_ss.at[step], info_rs.at[me8], pg, ps)
        copy.start()
        info_copies.append(copy)

    stage1, stage2 = [], []

    def start_first(j):
        for index in range(2):
            first = axes[index][0]
            for number, (pg, pc, near) in enumerate(((first, c, 1), (first, other, 1), (g, other, 0))):
                copy = remote(send[index][j].at[pc], pool[index][j].at[near, c],
                              s1s.at[j, index, number], s1r.at[j, index, near, c], pg, base + pc)
                copy.start()
                stage1.append(copy)

    def start_second(j):
        for index in range(2):
            first, second = axes[index]
            for near, cc in ((0, other), (1, 0), (1, 1)):
                remote(send[index][j].at[0], pool[index][j].at[near, cc], s1s.at[j, index, 0],
                       s1r.at[j, index, near, cc], first, s).wait_recv()
            for cc in range(CORES):
                source = info_s[second * CORES + cc, NBLK, 0] // seqs
                staged[index][j][cc] = pool[index][j][jnp.where(source == first, 1, 0), cc]
            copy = remote(staged[index][j], got[index][j], s2s.at[j, index], s2r.at[j, index], second, s)
            copy.start()
            stage2.append(copy)

    start_first(0)

    half_q = pl.ds(pl.multiple_of(c * HALFQ, HALFQ), HALFQ)
    away_q = pl.ds(pl.multiple_of(other * HALFQ, HALFQ), HALFQ)
    half_k = pl.ds(pl.multiple_of(c * HALF, HALF), HALF)
    away_k = pl.ds(pl.multiple_of(other * HALF, HALF), HALF)
    own_views = ((rq.at[:, half_q], qb), (rk.at[:, half_k], okb), (rv.at[:, half_k], ovb))
    away_views = ((rq.at[:, away_q], qb), (rk.at[:, away_k], okb), (rv.at[:, away_k], ovb), (qpb.at[c], qpb))
    q_local, q_remote = [], []
    for index, (src, buf) in enumerate(own_views):
        copy = pltpu.make_async_copy(src, buf.at[c], qls.at[index])
        copy.start()
        q_local.append(copy)
    for index, (src, buf) in enumerate(away_views):
        copy = remote(src, buf.at[c], qs.at[index], qr.at[index], g, base + other)
        copy.start()
        q_remote.append(copy)

    out_copies = []

    def passage(j):
        keys = jnp.concatenate([pk[b, :, j * HD : (j + 1) * HD] for b in range(NBLK)], axis=0)
        values = with_ones(
            jnp.concatenate([pv[b, :, j * HD : (j + 1) * HD] for b in range(NBLK)], axis=0)
        )

        def heads(pair, carry):
            for k in range(2):
                head = j * GQ + pair * 2 + k
                cols = pl.ds(pl.multiple_of(head * HD, HD), HD)
                for first in range(0, PLEN, QB):
                    rows = slice(first, first + QB)
                    pbuf[rows, cols] = passage_head(pq[rows, cols], keys, values, first)
            return carry

        lax.fori_loop(0, GQ // 2, heads, 0)
        cols = slice(j * GQ * HD, (j + 1) * GQ * HD)
        copy = pltpu.make_async_copy(pbuf.at[:, cols], pout.at[:, cols], outs.at[j])
        copy.start()
        out_copies.append(copy)

    passage(0)

    for step, pg, ps in peers():
        them = pg * CORES + lax.rem(c + step % CORES, CORES)
        remote(info.at[them], info.at[them], info_ss.at[step], info_rs.at[them], pg, ps).wait_recv()
    scalars = pltpu.make_async_copy(info, info_s, isem)
    scalars.start()
    scalars.wait()
    start_second(0)
    offset = lax.broadcasted_iota(jnp.int32, (8, BLK), 1)
    for cc in range(CORES):
        wanted = info_s[g * CORES + cc, NBLK, 0] // seqs
        slots = kept_slots([info_s[wanted * CORES + cc, i, 0] for i in range(NBLK)])
        for slot in range(KEEP):
            begin = jnp.where(slots[slot] >= 0, (base + cc) * PLEN + slots[slot] * BLK, FAR)
            first_lane = cc * ROWS + slot * BLK
            pos[z, :, first_lane : first_lane + BLK] = offset + begin

    def chain(zz, j):
        up = lax.rem(s + CORES, seqs)
        copies = [remote(kv.at[zz, j], kv.at[zz, j], chs.at[zz, j], chr_.at[zz, j], g, up)]
        if j == 0:
            copies.append(remote(pos.at[zz], pos.at[zz], chs.at[zz, HKV], chr_.at[zz, HKV], g, up))
        return copies

    def forward(zz, j):
        @pl.when(z < chips - 1)
        def _():
            for copy in chain(zz, j):
                copy.start()

    def finish_stage(j):
        for index in range(2):
            first = axes[index][0]
            stage2[2 * j + index].wait_recv()
            for cc in range(CORES):
                source = info_s[g * CORES + cc, NBLK, 0] // seqs
                near = pool[index][j][jnp.where(source == first, 1, 0), cc]
                here = (source == g) | (source == first)
                kv[z, j, index, cc * ROWS : (cc + 1) * ROWS] = jnp.where(here, near, got[index][j][cc])
        forward(z, j)

    passage(1)
    finish_stage(0)
    start_first(1)
    passage(2)
    start_second(1)
    passage(3)
    finish_stage(1)

    for copy in q_local:
        copy.wait()
    for copy in q_remote:
        copy.wait()
    queries_total = CORES * count

    def head_cols(j, h):
        return slice((j * GQ + h) * HD, (j * GQ + h + 1) * HD)

    def pair_queries(j, h):
        parts = [qb[cc, :, head_cols(j, h + k)] for k in range(2) for cc in range(CORES)]
        return jnp.concatenate(parts, axis=0)

    width = 2 * queries_total
    for j in range(HKV):
        cols = slice(j * HD, (j + 1) * HD)
        own_k = jnp.concatenate([okb[0, :, cols], okb[1, :, cols]] * 2, axis=0).astype(jnp.float32)
        own_v = jnp.concatenate([ovb[0, :, cols], ovb[1, :, cols]] * 2, axis=0).astype(jnp.float32)
        for h in range(0, GQ, 2):
            rows = slice(h * queries_total, h * queries_total + width)
            product = pair_queries(j, h).astype(jnp.float32) * own_k
            score = jnp.sum(product, axis=-1, keepdims=True)
            m_ref[j, rows] = jnp.broadcast_to(score, (width, HD))
            acc_ref[j, rows, :HD] = own_v
            acc_ref[j, rows, HD:] = jnp.ones((width, HD), jnp.float32)

    def absorb(zz, j):
        keys_pos = pos[zz, 0:1, :]
        query_pos = jnp.concatenate([qpb[0, :, 0:1], qpb[1, :, 0:1]], axis=0)
        bias = jnp.where(keys_pos < query_pos, 0.0, NEG).astype(jnp.float32)
        bias = jnp.concatenate([bias, bias], axis=0)
        keys = kv[zz, j, 0]
        values = with_ones(kv[zz, j, 1])
        for h in range(0, GQ, 2):
            rows = slice(h * queries_total, h * queries_total + width)
            scores = dot_nt(pair_queries(j, h), keys) + bias
            old = m_ref[j, rows]
            new = jnp.maximum(old, jnp.max(scores, axis=-1, keepdims=True))
            factor = jnp.exp2((old - new) * SCALE2)
            tiled = jnp.concatenate([new] * (CORES * KEEP), axis=1)
            weights = jnp.exp2((scores - tiled) * SCALE2).astype(jnp.bfloat16)
            mixture = jnp.dot(weights, values, preferred_element_type=jnp.float32)
            acc_ref[j, rows] = acc_ref[j, rows] * jnp.concatenate([factor, factor], axis=1) + mixture
            m_ref[j, rows] = new

    def visit(k, carry):
        zz = z - k

        for j in range(HKV):

            @pl.when(k > 0)
            def _():
                for copy in chain(zz, j):
                    copy.wait_recv()
                forward(zz, j)

            absorb(zz, j)
        return carry

    lax.fori_loop(0, z + 1, visit, 0)

    for j in range(HKV):
        for h in range(0, GQ, 2):
            rows = slice(h * queries_total, h * queries_total + width)
            result = (acc_ref[j, rows, :HD] / acc_ref[j, rows, HD:]).astype(jnp.bfloat16)
            for k in range(2):
                for cc in range(CORES):
                    first = k * queries_total + cc * count
                    ob[cc, :, head_cols(j, h + k)] = result[first : first + count]
    swap = remote(ob.at[other], ob.at[2], osem.at[0], osem.at[1], g, base + other)
    swap.start()
    mine = pltpu.make_async_copy(ob.at[c], rout.at[:, half_q], osem.at[2])
    mine.start()
    swap.wait_recv()
    theirs = pltpu.make_async_copy(ob.at[2], rout.at[:, away_q], osem.at[3])
    theirs.start()
    mine.wait()
    theirs.wait()
    swap.wait_send()

    for copy in out_copies:
        copy.wait()
    for copy in info_copies + stage1 + stage2:
        copy.wait_send()

    @pl.when(z < chips - 1)
    def _():
        def drain(zz, carry):
            for j in range(HKV):
                for copy in chain(zz, j):
                    copy.wait_send()
            return carry

        lax.fori_loop(0, z + 1, drain, 0)


def on_device(groups, seqs, passage_q, passage_k, passage_v, kept, context_map, recompute_pos,
              recompute_q, recompute_k, recompute_v):
    count = recompute_q.shape[1]
    chips = seqs // CORES
    bf, f32, i32 = jnp.bfloat16, jnp.float32, jnp.int32
    dma = pltpu.SemaphoreType.DMA
    smem = pl.BlockSpec(memory_space=pltpu.SMEM)
    vmem = pl.BlockSpec(memory_space=pltpu.VMEM)
    hbm = pl.BlockSpec(memory_space=pl.ANY)
    half = (CORES, ROWS, HD)
    heads_rows = GQ * CORES * count
    passage_out, reader_out = pl.pallas_call(
        functools.partial(kernel, groups, seqs),
        out_shape=(
            jax.ShapeDtypeStruct((PLEN, HQ * HD), bf),
            jax.ShapeDtypeStruct((count, HQ * HD), bf),
        ),
        in_specs=[smem, smem, smem, vmem, vmem, vmem, hbm, hbm, hbm],
        out_specs=(hbm, hbm),
        scratch_shapes=[
            pltpu.VMEM((chips, HKV, 2, CORES * ROWS, HD), bf),
            pltpu.VMEM((chips, 8, CORES * ROWS), i32),
            pltpu.VMEM((groups * CORES, 8, 128), i32),
            pltpu.SMEM((groups * CORES, 8, 128), i32),
            pltpu.VMEM((CORES, count, HALFQ), bf),
            pltpu.VMEM((CORES + 1, count, HALFQ), bf),
            pltpu.VMEM((CORES, count, HALF), bf),
            pltpu.VMEM((CORES, count, HALF), bf),
            pltpu.VMEM((CORES, count, HD), i32),
            pltpu.VMEM((HKV, heads_rows, HD), f32),
            pltpu.VMEM((HKV, heads_rows, 2 * HD), f32),
            pltpu.VMEM((PLEN, HQ * HD), bf),
            dma((2 * groups,)), dma((2 * groups,)),
            dma((HKV, 2, 3)), dma((HKV, 2, 2, CORES)),
            dma((HKV, 2)), dma((HKV, 2)),
            dma((chips, HKV + 1)), dma((chips, HKV + 1)),
            dma((4,)), dma((4,)), dma((4,)), dma((4,)), dma((KVH,)), dma,
        ]
        + [pltpu.VMEM(shape, bf) for shape in (half, (2,) + half, half, half) for _ in range(2 * HKV)],
        compiler_params=pltpu.CompilerParams(
            collective_id=0, has_side_effects=True, vmem_limit_bytes=56 * 2**20
        ),
        cost_estimate=pl.CostEstimate(
            flops=16 * 10**9, bytes_accessed=12 * 10**6, transcendentals=12 * 10**6
        ),
    )(
        kept, context_map, recompute_pos, passage_q,
        passage_k.reshape(NBLK, BLK, WKV), passage_v.reshape(NBLK, BLK, WKV),
        recompute_q[0], recompute_k[0], recompute_v[0],
    )
    return passage_out, reader_out[None]


def solution(mesh):
    both = P(("grp", "seq"), None)
    rows = P("grp", "seq", None)
    return jax.shard_map(
        functools.partial(on_device, mesh.shape["grp"], mesh.shape["seq"]),
        mesh=mesh,
        in_specs=(both, both, both, both, P("grp", "seq"), P("grp", "seq"), rows, rows, rows),
        out_specs=(both, rows),
        check_vma=False,
    )
```
